128 devices in a mesh: sky: 16 (over y, z), zb: 8 (over x, core).
Axes of the slice: x: 4, y: 4, z: 4, core: 2. Of those that a mesh axis runs over, the one named last changes fastest.
Arguments:
- stamps: bfloat16 [65536, 5120], P(('sky', 'zb')), may hold values from -6 to 6
- counts: int32 [128], P(('sky', 'zb')), may hold values from 1 to 512, 49152 in all
- dest: int32 [65536, 1], P(('sky', 'zb')), may hold values from 0 to 127; in each aligned block of 512 rows (0 to 511, 512 to 1023, ...) at most 8 rows name the same one
- pixel_ids: int32 [65536], P(('sky', 'zb')), may hold values from 0 to 1023
- conv1_w: bfloat16 [3, 3, 5, 64], replicated, may hold values from -1.25 to 1.25
- conv2_w: bfloat16 [3, 3, 32, 128], replicated, may hold values from -0.5 to 0.5
- conv3_w: bfloat16 [3, 3, 64, 256], replicated, may hold values from -0.375 to 0.375
- dense_w: bfloat16 [4096, 512], replicated, may hold values from -0.125 to 0.125
- head_w: bfloat16 [512, 48], replicated, may hold values from -0.25 to 0.25
Outputs:
- pdf_rows: bfloat16 [131072, 512], P(('sky', 'zb'))
- nz_map: float32 [1024, 512], P('sky', 'zb')
The draws below stay inside these ranges and needn't reach their ends.
Inputs may be any that keep to these rules, and one draw needn't show every extreme that they name: `dest`: in the rows of one tile owner no worker is named more than 8 times.
All inputs are finite; a program needn't handle non-finite values. No bound on the sum of `counts` on one device may be relied on, other than what follows from the above.
Results may differ from the reference program's by a relative error of at most 0.012.
Values may be sent and summed in bfloat16 or wider, within the bound.
No kernel may reach another device: no remote copies, remote signals or barrier semaphores. Data moves between devices by JAX's collectives and lax.ppermute only.
A program may use at most 384 MiB of HBM per device.

```python
import math
import jax
import jax.numpy as jnp
import numpy as np
from jax import lax

STAMP_DEV = 512
NBIN = 512
NCOMP = 16
BANDS = 5
STAMP = 32
C1 = 64
C2 = 128
C3 = 256
HIDDEN_SIZE = 512
GROUPS = 2
CAP = 8
SLOTS = 1024
GALAXIES = 65536
NPIX = 1024
DEVICES = 128


def set_ends(values, rng, smallest, top_value):
    longest = values.shape.index(max(values.shape))
    spots = []
    for shift in (0, 1):
        where = [jax.random.randint(jax.random.fold_in(rng, axis), (), 0, length) for axis, length in enumerate(values.shape)]
        where[longest] = (where[longest] + shift) % values.shape[longest]
        spots.append(tuple(where))
    return values.at[spots[0]].set(smallest).at[spots[1]].set(top_value)


def block_levels(stream_key, extent, pieces, smallest, high):
    loudness, own = 1.0, jax.random.fold_in(stream_key, 6)
    for dim, shards_of in pieces:
        heights = jnp.exp(jax.random.uniform(jax.random.fold_in(own, dim), (shards_of,), jnp.float32, smallest / len(pieces), high / len(pieces)))
        loudness = loudness * jnp.repeat(heights, extent[dim] // shards_of).reshape([-1 if axis == dim else 1 for axis in range(len(extent))])
    return loudness


def profile(number_of, total, most, lean):
    portions = [(1 << 20) // math.isqrt(rank ** lean) + 1 for rank in range(2, number_of + 1)]
    spare, holding = total - most - (number_of - 1), [1] * (number_of - 1)
    while spare > 0:
        candidates = [i for i in range(number_of - 1) if holding[i] < most]
        whole, remaining = sum([portions[i] for i in candidates]), spare
        for i in candidates:
            extra = min(most - holding[i], max(1, remaining * portions[i] // whole), spare)
            holding[i] = holding[i] + extra
            spare = spare - extra
    return np.array([most] + holding)


def ragged(own_key, count, total, most, lean):
    if count == 2:
        one = jax.random.randint(own_key, (), max(1, total - most), min(most, total - 1) + 1)
        return jnp.stack([one, total - one])
    tallies = jnp.asarray(profile(count, total, most, lean), jnp.int32)
    twos = (count - 1) // 2
    giver, taker = tallies[1:1 + 2 * twos:2], tallies[2:2 + 2 * twos:2]
    slack = jnp.minimum(giver - 1, most - taker)
    moved = jax.random.randint(jax.random.fold_in(own_key, 1), (twos,), 0, 1 << 20) % (slack + 1)
    tallies = tallies.at[1:1 + 2 * twos:2].set(giver - moved).at[2:2 + 2 * twos:2].set(taker + moved)
    return tallies[jax.random.permutation(jax.random.fold_in(own_key, 2), count)]


def routed_block(stream_key, own, number, rows, number_of, top, limit, skew):
    order = jax.random.permutation(stream_key, number_of)
    crowded, ordinary = portions_of(number_of, rows * top, limit, skew, True), portions_of(number_of, rows * top, limit, skew, False)
    places = jnp.arange(number_of)

    def named(lengths, turn):
        used = int((lengths > 0).sum())
        fixed = max(1, used // 4)
        moved = fixed + (places - fixed + turn * (used - fixed)) % max(1, number_of - fixed)
        return jnp.zeros((number_of,), jnp.int32).at[order[jnp.where(places < fixed, places, moved)]].set(jnp.asarray(lengths, jnp.int32))

    lengths = jnp.where(number % 4 == 0, named(crowded, number // 4), named(ordinary, number - number // 4 - 1))
    mixed = jax.random.permutation(jax.random.fold_in(own, 3), number_of)
    donor, sink = mixed[0:number_of // 2 * 2:2], mixed[1:number_of // 2 * 2:2]
    slack = jnp.minimum(lengths[donor] - 1, limit - lengths[sink]) // 2
    slack = jnp.where((donor == order[0]) | (sink == order[0]) | (lengths[sink] == 0), 0, jnp.maximum(slack, 0))
    moved = jax.random.randint(jax.random.fold_in(own, 4), (number_of // 2,), 0, 1 << 20) % (slack + 1)
    lengths = lengths.at[donor].add(-moved).at[sink].add(moved)
    labels = jnp.searchsorted(jnp.cumsum(lengths), jnp.arange(rows * top), side="right").astype(jnp.int32)
    grid = labels.reshape(top, rows).T
    grid = grid[jax.random.permutation(jax.random.fold_in(own, 1), rows)]
    turn = jax.random.randint(jax.random.fold_in(own, 2), (rows, 1), 0, top)
    return jnp.take_along_axis(grid, (jnp.arange(top)[None, :] + turn) % top, axis=1)


def portions_of(count, total, most, lean, full):
    portions = [(1 << 20) // math.isqrt(rank ** lean) + 1 for rank in range(1, count + 1)]
    largest = most if full else min(most, max(-(-total // count), total * portions[0] // sum(portions)))
    least = 1 if total - largest >= count - 1 else 0
    given, spare = [largest] + [least] * (count - 1), total - largest - least * (count - 1)
    while spare > 0:
        movable = [i for i in range(1, count) if given[i] < largest] or [i for i in range(1, count) if given[i] < most]
        mass, budget = sum([portions[i] for i in movable]), spare
        for i in movable:
            addition = min(most - given[i], max(1, budget * portions[i] // mass), spare)
            given[i] = given[i] + addition
            spare = spare - addition
    return np.array(given)


def scatter_about(own_key, dims, scale, bound, shards=(), kind=jnp.bfloat16):
    gain = block_levels(own_key, dims, shards, -0.22, 0.18) if shards else 1.0
    drawn = jax.random.normal(own_key, dims, jnp.float32) * scale * gain
    return jnp.minimum(jnp.maximum(drawn, -bound), bound).astype(kind)


def setup_inputs(seed: int = 0) -> dict:
    seeds = jax.random.split(jax.random.key(seed), 10)
    stamps = scatter_about(seeds[0], (GALAXIES, STAMP * STAMP * BANDS), 1.0, 6.0, ((0, 128),))
    counts = ragged(seeds[1], DEVICES, 3 * STAMP_DEV * DEVICES // 4, STAMP_DEV, 2).astype(jnp.int32)
    dest_keys = jax.random.split(jax.random.fold_in(seeds[2], 1), GALAXIES // STAMP_DEV)
    dest_turns = jax.random.permutation(jax.random.fold_in(seeds[2], 3), GALAXIES // STAMP_DEV)
    dest = jax.vmap(lambda own, number: routed_block(jax.random.fold_in(seeds[2], 2), own, number, STAMP_DEV, DEVICES, 1, CAP, 2))(dest_keys, dest_turns).reshape((GALAXIES, 1))
    pixel_ids = set_ends(jax.random.randint(seeds[3], (GALAXIES,), 0, NPIX), jax.random.fold_in(seeds[3], 1), 0, NPIX - 1).astype(jnp.int32)
    conv1_w = scatter_about(seeds[4], (3, 3, BANDS, C1), (BANDS * 9 // 2) ** -0.5, 1.25)
    conv2_w = scatter_about(seeds[5], (3, 3, C1 // GROUPS, C2), (C1 * 9 // (2 * GROUPS)) ** -0.5, 0.5)
    conv3_w = scatter_about(seeds[6], (3, 3, C2 // GROUPS, C3), (C2 * 9 // (2 * GROUPS)) ** -0.5, 0.375)
    dense_w = scatter_about(seeds[7], (C3 * (STAMP // 8) * (STAMP // 8), HIDDEN_SIZE), (C3 * (STAMP // 8) * (STAMP // 8) // 2) ** -0.5, 0.125)
    head_w = scatter_about(seeds[8], (HIDDEN_SIZE, 3 * NCOMP), HIDDEN_SIZE ** -0.5, 0.25)
    return {"stamps": stamps, "counts": counts, "dest": dest, "pixel_ids": pixel_ids, "conv1_w": conv1_w, "conv2_w": conv2_w, "conv3_w": conv3_w, "dense_w": dense_w, "head_w": head_w}


Z_TOP = 3.0
SPREAD_LOW = 0.05
SPREAD_RANGE = 0.25

def convolve(images, kernel, groups):
    return lax.conv_general_dilated(images.astype(jnp.float32), kernel.astype(jnp.float32), (2, 2), ((1, 1), (1, 1)), dimension_numbers=('NHWC', 'HWIO', 'NHWC'), feature_group_count=groups, precision=lax.Precision.HIGHEST)

def mixture(head_out, bin_total):
    logits = head_out[:, :NCOMP]
    centres = Z_TOP * jax.nn.sigmoid(head_out[:, NCOMP:2 * NCOMP])
    spreads = SPREAD_LOW + SPREAD_RANGE * jax.nn.sigmoid(head_out[:, 2 * NCOMP:])
    shares = jax.nn.softplus(logits) + 0.1
    shares = shares / lax.optimization_barrier(jnp.sum(shares, axis=1, keepdims=True))
    bin_edges = Z_TOP * jnp.arange(bin_total + 1, dtype=jnp.float32) / bin_total
    scaled = (bin_edges[None, None, :] - centres[:, :, None]) / (spreads[:, :, None] * math.sqrt(2.0))
    cumulative = 0.5 * (1.0 + lax.erf(scaled))
    masses = cumulative[:, :, 1:] - cumulative[:, :, :-1]
    return lax.optimization_barrier(jnp.sum(shares[:, :, None] * masses, axis=1))

def network(images, conv1_w, conv2_w, conv3_w, dense_w, head_w):
    amount = images.shape[0]
    stamp_grid = images.reshape(amount, STAMP, STAMP, BANDS)
    layer_one = jax.nn.relu(convolve(stamp_grid, conv1_w, 1)).astype(jnp.bfloat16)
    layer_two = jax.nn.relu(convolve(layer_one, conv2_w, GROUPS)).astype(jnp.bfloat16)
    layer_three = jax.nn.relu(convolve(layer_two, conv3_w, GROUPS)).astype(jnp.bfloat16)
    hidden = jax.nn.relu(jnp.dot(layer_three.reshape(amount, -1), dense_w, preferred_element_type=jnp.float32)).astype(jnp.bfloat16)
    head_out = jnp.dot(hidden, head_w, preferred_element_type=jnp.float32)
    return mixture(head_out, NBIN)

def reference(stamps, counts, dest, pixel_ids, conv1_w, conv2_w, conv3_w, dense_w, head_w):
    blocks = stamps.reshape(DEVICES, STAMP_DEV, stamps.shape[1])
    density = lax.map(lambda block: network(block, conv1_w, conv2_w, conv3_w, dense_w, head_w), blocks)
    row_order = jnp.arange(STAMP_DEV, dtype=jnp.int32)
    is_valid = row_order[None, :] < counts[:, None]
    density = jnp.where(is_valid[:, :, None], density, 0.0).astype(jnp.bfloat16)
    targets = dest.reshape(DEVICES, STAMP_DEV)
    before = (targets[:, :, None] == targets[:, None, :]) & (row_order[None, None, :] < row_order[None, :, None])
    slot_rank = lax.optimization_barrier(jnp.sum(before.astype(jnp.int32), axis=2)).astype(jnp.int32)
    sources = jnp.arange(DEVICES, dtype=jnp.int32)[:, None]
    row_index = (targets * SLOTS + sources * CAP + slot_rank).reshape(-1).astype(jnp.int32)
    flat_density = density.reshape(-1, NBIN)
    pdf_rows = jnp.zeros((DEVICES * SLOTS, NBIN), jnp.bfloat16).at[row_index].set(flat_density)
    nz_map = jax.ops.segment_sum(flat_density.astype(jnp.float32), pixel_ids.reshape(-1), num_segments=NPIX)
    return (pdf_rows, nz_map)
```

```python
import math

import jax
import jax.numpy as jnp
from jax import lax
from jax.sharding import PartitionSpec as P

NBIN = 512
NCOMP = 16
BANDS = 5
STAMP = 32
GROUPS = 2
NPIX = 1024


Z_TOP = 3.0
SPREAD_LOW = 0.05
SPREAD_RANGE = 0.25


def convolve(images, kernel, groups):
    return lax.conv_general_dilated(
        images,
        kernel,
        (2, 2),
        ((1, 1), (1, 1)),
        dimension_numbers=("NHWC", "HWIO", "NHWC"),
        feature_group_count=groups,
        preferred_element_type=jnp.float32,
    )


def mixture(head_out, bin_total):
    logits = head_out[:, :NCOMP]
    centres = Z_TOP * jax.nn.sigmoid(head_out[:, NCOMP : 2 * NCOMP])
    spreads = SPREAD_LOW + SPREAD_RANGE * jax.nn.sigmoid(head_out[:, 2 * NCOMP :])
    shares = jax.nn.softplus(logits) + 0.1
    shares = shares / jnp.sum(shares, axis=1, keepdims=True)
    bin_edges = Z_TOP * jnp.arange(bin_total + 1, dtype=jnp.float32) / bin_total
    scaled = (bin_edges[None, None, :] - centres[:, :, None]) / (
        spreads[:, :, None] * math.sqrt(2.0)
    )
    cumulative = 0.5 * (1.0 + lax.erf(scaled))
    masses = cumulative[:, :, 1:] - cumulative[:, :, :-1]
    return jnp.sum(shares[:, :, None] * masses, axis=1)


def network(images, conv1_w, conv2_w, conv3_w, dense_w, head_w):
    amount = images.shape[0]
    stamp_grid = images.reshape(amount, STAMP, STAMP, BANDS)
    layer_one = jax.nn.relu(convolve(stamp_grid, conv1_w, 1)).astype(jnp.bfloat16)
    layer_two = jax.nn.relu(convolve(layer_one, conv2_w, GROUPS)).astype(jnp.bfloat16)
    layer_three = jax.nn.relu(convolve(layer_two, conv3_w, GROUPS)).astype(jnp.bfloat16)
    hidden = jax.nn.relu(
        jnp.dot(layer_three.reshape(amount, -1), dense_w, preferred_element_type=jnp.float32)
    ).astype(jnp.bfloat16)
    head_out = jnp.dot(hidden, head_w, preferred_element_type=jnp.float32)
    return mixture(head_out, NBIN)


def local(stamps, counts, dest, pixel_ids, conv1_w, conv2_w, conv3_w, dense_w, head_w):
    devices = lax.axis_size(("sky", "zb"))
    zb_size = lax.axis_size("zb")
    sky_size = lax.axis_size("sky")
    row_total = stamps.shape[0]
    capacity = max(2, 2 * row_total // devices)
    slot_total = devices * capacity
    bin_share = NBIN // zb_size
    pix_share = NPIX // sky_size
    row_order = jnp.arange(row_total, dtype=jnp.int32)
    is_valid = row_order < counts[0]
    target = dest[:, 0]
    before = (target[:, None] == target[None, :]) & (row_order[None, :] < row_order[:, None])
    slot_rank = jnp.sum(before.astype(jnp.int32), axis=1)
    position = target * capacity + slot_rank
    density = network(stamps, conv1_w, conv2_w, conv3_w, dense_w, head_w)
    density = jnp.where(is_valid[:, None], density, 0.0).astype(jnp.bfloat16)
    place = (jnp.arange(slot_total, dtype=jnp.int32)[:, None] == position[None, :]).astype(
        jnp.bfloat16
    )
    pdf_send = jnp.dot(place, density, preferred_element_type=jnp.float32).astype(jnp.bfloat16)
    pdf_send = pdf_send.reshape(devices, capacity, NBIN)
    pair = (jnp.arange(NPIX // 2, dtype=jnp.int32)[:, None] == (pixel_ids // 2)[None, :]).astype(
        jnp.bfloat16
    )
    odd = (pixel_ids % 2 == 1)[:, None, None]
    split = density.reshape(row_total, zb_size, bin_share)
    zero = jnp.zeros_like(split)
    both = jnp.stack([jnp.where(odd, zero, split), jnp.where(odd, split, zero)], axis=2)
    partial = jnp.dot(
        pair, both.reshape(row_total, 2 * NBIN), preferred_element_type=jnp.float32
    ).astype(jnp.bfloat16)
    map_send = partial.reshape(sky_size, pix_share // 2, zb_size, 2 * bin_share)
    map_send = map_send.transpose(0, 2, 1, 3).reshape(devices, capacity, NBIN)
    received = lax.all_to_all(
        jnp.concatenate([pdf_send, map_send], axis=1),
        ("sky", "zb"),
        split_axis=0,
        concat_axis=0,
        tiled=True,
    )
    pdf_rows = received[:, :capacity].reshape(slot_total, NBIN)
    nz_map = jnp.sum(received[:, capacity:].astype(jnp.float32), axis=0)
    return (pdf_rows, nz_map.reshape(pix_share, bin_share))


def solution(mesh):
    in_specs = (
        P(("sky", "zb"), None),
        P(("sky", "zb")),
        P(("sky", "zb"), None),
        P(("sky", "zb")),
        P(),
        P(),
        P(),
        P(),
        P(),
    )
    out_specs = (P(("sky", "zb"), None), P("sky", "zb"))
    return jax.shard_map(local, mesh=mesh, in_specs=in_specs, out_specs=out_specs, check_vma=False)
```

```python
import functools
import math

import jax
import jax.numpy as jnp
from jax import lax
from jax.experimental import pallas as pl
from jax.experimental.pallas import tpu as pltpu
from jax.sharding import PartitionSpec as P

ROWS = 512
NBIN = 512
NCOMP = 16
BANDS = 5
STAMP = 32
PIXELS = STAMP * STAMP * BANDS
NPIX = 1024
C1 = 64
C2 = 128
C3 = 256
HIDDEN = 512
CAP = 8
DEVICES = 128
SKY = 16
ZB = 8
PIX_DEV = NPIX // SKY
BIN_DEV = NBIN // ZB
MAP_ROWS = PIX_DEV * BIN_DEV // 128
BLOCK = MAP_ROWS + CAP
FRONT = 256
PITCH = 1024
EDGE_ROWS = 520

Z_TOP = 3.0
SPREAD_LOW = 0.05
SPREAD_RANGE = 0.25

F32 = jnp.float32
BF16 = jnp.bfloat16


def iota(shape, dim):
    return lax.broadcasted_iota(jnp.int32, shape, dim)


def relu16(values):
    return jnp.maximum(values, 0.0).astype(BF16)


def dot(left, right):
    return jnp.dot(left, right, preferred_element_type=F32)


def dot_nt(left, right):
    return lax.dot_general(left, right, (((1,), (1,)), ((), ())), preferred_element_type=F32)


def spread_first(w1_ref, w1_s, t1_s):
    w1_s[...] = jnp.zeros_like(w1_s)
    for kh in range(3):
        for kw in range(3):
            w1_s[kw, pl.ds(kh * BANDS, BANDS), :] = w1_ref[kh, kw].astype(F32)
    chan, lane = iota((C1, 512), 0), iota((C1, 512), 1)
    repeat = (chan == (lane >= 256) * 32 + (lane & 31)).astype(F32).astype(BF16)

    def row_parts(shape):
        k = iota(shape, 0)
        kh = (k >= 85).astype(jnp.int32) + (k >= 170).astype(jnp.int32)
        rem = k - 85 * kh
        col = (rem * 205) >> 10
        return k, kh, col, rem - 5 * col

    k, kh, col, band = row_parts((256, 16))
    pick = ((iota((256, 16), 1) == kh * BANDS + band) & (k < 255)).astype(F32).astype(BF16)
    k, kh, col, band = row_parts((256, 512))
    tap = col - 2 * ((iota((256, 512), 1) & 255) >> 5)
    total = jnp.zeros((256, 512), F32)
    for kw in range(3):
        lanes = dot(w1_s[kw].astype(BF16), repeat).astype(BF16)
        total = jnp.where(tap == kw, dot(pick, lanes), total)
    t1_s[1] = total.astype(BF16)
    t1_s[0] = jnp.where(col == 0, 0.0, total).astype(BF16)


def spread_second(w2_ref, w2a_s, w2b_s):
    w2a_s[...] = jnp.zeros_like(w2a_s)
    w2b_s[...] = jnp.zeros_like(w2b_s)
    low = iota((32, 128), 1) < 64
    zero = jnp.zeros((32, 128), F32)
    for kh in range(3):
        plain = [w2_ref[kh, kw].astype(F32) for kw in range(3)]
        swapped = [pltpu.roll(tap, 64, 1) for tap in plain]
        for g in range(2):
            lo = plain if g == 0 else swapped
            hi = swapped if g == 0 else plain
            for d in range(-1, 4):
                first = lo[d + 1] if d + 1 <= 2 else zero
                second = hi[d - 1] if d >= 1 else zero
                tile = jnp.where(low, first, second).astype(BF16)
                for q in range(2):
                    c = d + 4 * q
                    if -1 <= c <= 7:
                        at = kh * 384 + 128 + 32 * c
                        w2b_s[g, at : at + 32, 128 * q : 128 * q + 128] = tile
                    if 0 <= c <= 7:
                        at = kh * 256 + 32 * c
                        w2a_s[g, at : at + 32, 128 * q : 128 * q + 128] = tile


def spread_third(w3_ref, w3a_s, w3b_s):
    w3a_s[...] = jnp.zeros_like(w3a_s)
    w3b_s[...] = jnp.zeros_like(w3b_s)
    for kh in range(3):
        for kw in range(3):
            for g in range(2):
                tap = w3_ref[kh, kw, :, g * 128 : g * 128 + 128]
                for oc in range(2):
                    c = kw + 2 * oc - 1
                    at = kh * 384 + 128 + 64 * c
                    w3b_s[g, at : at + 64, 128 * oc : 128 * oc + 128] = tap
                    if c >= 0:
                        at = kh * 256 + 64 * c
                        w3a_s[g, at : at + 64, 128 * oc : 128 * oc + 128] = tap


def grouped(source, row, wa_s, wb_s, store):
    for g in range(2):
        for half in range(2):
            width = 384 if half else 256
            parts = []
            for kh in range(3):
                at = pl.multiple_of((2 * row + kh) * PITCH, PITCH) + (g * 512 + half * 128)
                parts.append(source[:, pl.ds(pl.multiple_of(at, 128), width)])
            weights = wb_s[g] if half else wa_s[g]
            store(g, half, relu16(dot(jnp.concatenate(parts, axis=1), weights)))


def coefficients(logits, mids, widths, axis, live):
    share = jnp.maximum(logits, 0.0) + jnp.log1p(jnp.exp(-jnp.abs(logits))) + 0.1
    return share, Z_TOP * jax.nn.sigmoid(mids), 1.0 / (
        (SPREAD_LOW + SPREAD_RANGE * jax.nn.sigmoid(widths)) * math.sqrt(2.0)
    )


def owner_kernel(
    counts_ref, dest_ref, pixel_ref, x_hbm, w1_ref, w2_ref, w3_ref, wd_hbm, wh_ref,
    send_ref,
    x_s, wd_s, l1_s, l2_s, l3_s, w1_s, t1_s, w2a_s, w2b_s, w3a_s, w3b_s, coef_s, cdf_s, den_s,
    sems,
):
    x_copy = pltpu.make_async_copy(x_hbm, x_s.at[:, pl.ds(FRONT, PIXELS)], sems.at[0])
    x_copy.start()
    d_copy = pltpu.make_async_copy(wd_hbm, wd_s, sems.at[1])
    d_copy.start()
    x_s[:, 0:FRONT] = jnp.zeros((ROWS, FRONT), BF16)
    l1_s[:, 0:PITCH] = jnp.zeros((ROWS, PITCH), BF16)
    l2_s[:, 0:PITCH] = jnp.zeros((ROWS, PITCH), BF16)
    spread_first(w1_ref, w1_s, t1_s)
    spread_second(w2_ref, w2a_s, w2b_s)
    spread_third(w3_ref, w3a_s, w3b_s)
    x_copy.wait()

    def first(t, carry):
        x = x_s[:, pl.ds(pl.multiple_of(t * 640, 128), 896)]
        for odd in range(2):
            for half in range(2):
                start = 91 + 320 * odd + 80 * half
                window = jnp.concatenate(
                    [x[:, start + 160 * kh : start + 160 * kh + 85] for kh in range(3)]
                    + [jnp.zeros((ROWS, 1), BF16)],
                    axis=1,
                )
                out = relu16(dot(window, t1_s[half]))
                at = pl.multiple_of((2 * t + odd + 1) * PITCH, PITCH)
                for g in range(2):
                    l1_s[:, pl.ds(pl.multiple_of(at + (g * 512 + half * 256), 128), 256)] = out[
                        :, g * 256 : g * 256 + 256
                    ]
        return carry

    lax.fori_loop(0, STAMP // 4, first, 0)

    def second(r, carry):
        def store(g, half, out):
            at = pl.multiple_of((r + 1) * PITCH, PITCH) + (g * 512 + half * 256)
            l2_s[:, pl.ds(pl.multiple_of(at, 128), 256)] = out

        grouped(l1_s, r, w2a_s, w2b_s, store)
        return carry

    lax.fori_loop(0, STAMP // 4, second, 0)

    def third(r, carry):
        def store(g, half, out):
            for oc in range(2):
                at = pl.multiple_of(r * 1024, 1024) + ((2 * half + oc) * 256 + g * 128)
                l3_s[:, pl.ds(pl.multiple_of(at, 128), 128)] = out[:, oc * 128 : oc * 128 + 128]

        grouped(l2_s, r, w3a_s, w3b_s, store)
        return carry

    lax.fori_loop(0, STAMP // 8, third, 0)
    d_copy.wait()
    hidden = relu16(dot(l3_s[...], wd_s[...]))
    wh = wh_ref[...]
    head = dot(hidden, jnp.concatenate([wh, wh, jnp.zeros((HIDDEN, 32), BF16)], axis=1))

    count = counts_ref[0]
    high = head.astype(BF16).astype(F32)
    lane = iota((ROWS, 128), 1)
    alive = (iota((ROWS, 128), 0) < count).astype(F32)
    params = jnp.where(lane < 48, high, jnp.where(lane < 96, head - high, alive)).astype(BF16)
    dest = dest_ref[...]
    named = iota((DEVICES, ROWS), 0) == dest
    named16 = named.astype(F32).astype(BF16)
    earlier = (iota((ROWS, ROWS), 0) < iota((ROWS, ROWS), 1)).astype(F32).astype(BF16)
    rank = jnp.sum(jnp.where(named, dot(named16, earlier), 0.0), axis=0, keepdims=True)
    position = dest * CAP + rank.astype(jnp.int32)
    place = (iota((DEVICES * CAP, ROWS), 0) == position).astype(F32).astype(BF16)
    slots = dot(place, params).reshape(DEVICES, CAP, 128)
    send_ref[:, MAP_ROWS:BLOCK, :] = slots.astype(BF16)

    turned = head.T
    share, centre, inverse = coefficients(
        turned[0:16], turned[16:32], turned[32:48], 0, None
    )
    live = (iota((1, ROWS), 1) < count).astype(F32)
    coef_s[0] = share * (0.5 * live / jnp.sum(share, axis=0, keepdims=True))
    coef_s[1] = centre
    coef_s[2] = inverse
    blocks, depth = 5, EDGE_ROWS // 5

    def mix(step, carry):
        block, tile = step // 4, step % 4
        lanes = pl.ds(pl.multiple_of(tile * 128, 128), 128)
        rows = pl.multiple_of(block * depth, 8)
        edge = (iota((depth, 128), 0) + rows).astype(F32) * Z_TOP / NBIN
        total = jnp.zeros((depth, 128), F32)
        for k in range(NCOMP):
            scaled = (edge - coef_s[1, k : k + 1, lanes]) * coef_s[2, k : k + 1, lanes]
            total = total + coef_s[0, k : k + 1, lanes] * lax.erf(scaled)
        cdf_s[pl.ds(rows, depth), lanes] = total
        return carry

    lax.fori_loop(0, blocks * 4, mix, 0)
    density = (cdf_s[1 : NBIN + 1, :] - cdf_s[0:NBIN, :]).astype(BF16).astype(F32)

    pixel = pixel_ref[...]
    odd = (pixel & 1).astype(F32)
    for j in range(ZB):
        part = density[j * BIN_DEV : (j + 1) * BIN_DEV]
        den_s[j * 128 : j * 128 + 64, :] = (part * (1.0 - odd)).astype(BF16)
        den_s[j * 128 + 64 : j * 128 + 128, :] = (part * odd).astype(BF16)
    pair = (iota((NPIX // 2, ROWS), 0) == (pixel >> 1)).astype(F32).astype(BF16)
    for q in range(ZB // 2):
        maps = dot_nt(pair, den_s[q * 256 : q * 256 + 256, :]).astype(BF16)
        for s in range(SKY):
            for j in range(2):
                send_ref[s * ZB + 2 * q + j, 0:MAP_ROWS, :] = maps[
                    s * MAP_ROWS : (s + 1) * MAP_ROWS, j * 128 : j * 128 + 128
                ]


def owner(stamps, counts, dest, pixel_ids, conv1_w, conv2_w, conv3_w, dense_w, head_w):
    vmem = pl.BlockSpec(memory_space=pltpu.VMEM)
    hbm = pl.BlockSpec(memory_space=pl.ANY)
    return pl.pallas_call(
        owner_kernel,
        out_shape=jax.ShapeDtypeStruct((DEVICES, BLOCK, 128), BF16),
        in_specs=[pl.BlockSpec(memory_space=pltpu.SMEM), vmem, vmem, hbm, vmem, vmem, vmem, hbm, vmem],
        out_specs=vmem,
        scratch_shapes=[
            pltpu.VMEM((ROWS, FRONT + PIXELS), BF16),
            pltpu.VMEM((C3 * 16, HIDDEN), BF16),
            pltpu.VMEM((ROWS, 17 * PITCH), BF16),
            pltpu.VMEM((ROWS, 9 * PITCH), BF16),
            pltpu.VMEM((ROWS, C3 * 16), BF16),
            pltpu.VMEM((3, 16, C1), F32),
            pltpu.VMEM((2, 256, 512), BF16),
            pltpu.VMEM((2, 768, 256), BF16),
            pltpu.VMEM((2, 1152, 256), BF16),
            pltpu.VMEM((2, 768, 256), BF16),
            pltpu.VMEM((2, 1152, 256), BF16),
            pltpu.VMEM((3, NCOMP, ROWS), F32),
            pltpu.VMEM((EDGE_ROWS, ROWS), F32),
            pltpu.VMEM((2 * NBIN, ROWS), BF16),
            pltpu.SemaphoreType.DMA((2,)),
        ],
        compiler_params=pltpu.CompilerParams(vmem_limit_bytes=62 * 1024 * 1024),
        cost_estimate=pl.CostEstimate(
            flops=20_000_000_000, bytes_accessed=13_000_000, transcendentals=4_300_000
        ),
        name="owner",
    )(counts, dest.reshape(1, ROWS), pixel_ids.reshape(1, ROWS), stamps, conv1_w, conv2_w, conv3_w,
      dense_w, head_w)


def worker_kernel(got_ref, rows_ref, map_ref, coef_s, last_s):
    def add(i, total):
        part = got_ref[pl.ds(i * 8, 8), 0:MAP_ROWS, :].astype(F32)
        return total + jnp.sum(part, axis=0)

    total = lax.fori_loop(0, DEVICES // 8, add, jnp.zeros((MAP_ROWS, 128), F32))
    map_ref[pl.ds(0, PIX_DEV // 2, stride=2), :] = total[:, 0:64]
    map_ref[pl.ds(1, PIX_DEV // 2, stride=2), :] = total[:, 64:128]

    slots = DEVICES * CAP
    packed = got_ref[:, MAP_ROWS:BLOCK, :].astype(F32).reshape(slots, 128)
    head = packed + pltpu.roll(packed, 80, 1)
    live = packed[:, 96:97]
    lane = iota((slots, 128), 1)
    share = jnp.maximum(head, 0.0) + jnp.log1p(jnp.exp(-jnp.abs(head))) + 0.1
    share = jnp.where(lane < NCOMP, share, 0.0)
    share = share * (0.5 * live / jnp.sum(share, axis=1, keepdims=True))
    gate = jax.nn.sigmoid(head)
    centre = Z_TOP * pltpu.roll(gate, 112, 1)
    inverse = 1.0 / ((SPREAD_LOW + SPREAD_RANGE * pltpu.roll(gate, 96, 1)) * math.sqrt(2.0))
    coef_s[0] = share
    coef_s[1] = centre
    coef_s[2] = inverse
    last_s[...] = jnp.broadcast_to(
        jnp.sum(share * lax.erf((Z_TOP - centre) * inverse), axis=1, keepdims=True), (slots, 128)
    )
    high = 32

    def mix(step, carry):
        rows = pl.ds(pl.multiple_of(step * high, high), high)
        edge = iota((high, NBIN), 1).astype(F32) * Z_TOP / NBIN
        share, centre, inverse = coef_s[0, rows, :], coef_s[1, rows, :], coef_s[2, rows, :]
        total = jnp.zeros((high, NBIN), F32)
        for k in range(NCOMP):
            scaled = (edge - centre[:, k : k + 1]) * inverse[:, k : k + 1]
            total = total + share[:, k : k + 1] * lax.erf(scaled)
        after = pltpu.roll(total, NBIN - 1, 1)
        after = jnp.where(iota((high, NBIN), 1) == NBIN - 1, last_s[rows, 0:1], after)
        rows_ref[rows, :] = (after - total).astype(BF16)
        return carry

    lax.fori_loop(0, slots // high, mix, 0)


def worker(received):
    vmem = pl.BlockSpec(memory_space=pltpu.VMEM)
    slots = DEVICES * CAP
    return pl.pallas_call(
        worker_kernel,
        out_shape=(
            jax.ShapeDtypeStruct((slots, NBIN), BF16),
            jax.ShapeDtypeStruct((PIX_DEV, BIN_DEV), F32),
        ),
        in_specs=[vmem],
        out_specs=(vmem, vmem),
        scratch_shapes=[pltpu.VMEM((3, slots, 128), F32), pltpu.VMEM((slots, 128), F32)],
        compiler_params=pltpu.CompilerParams(vmem_limit_bytes=32 * 1024 * 1024),
        name="worker",
    )(received)


def local(*arrays):
    send = owner(*arrays)
    received = lax.all_to_all(send, ("sky", "zb"), split_axis=0, concat_axis=0, tiled=True)
    return worker(received)


def solution(mesh):
    in_specs = (
        P(("sky", "zb"), None),
        P(("sky", "zb")),
        P(("sky", "zb"), None),
        P(("sky", "zb")),
        P(),
        P(),
        P(),
        P(),
        P(),
    )
    out_specs = (P(("sky", "zb"), None), P("sky", "zb"))
    return jax.shard_map(local, mesh=mesh, in_specs=in_specs, out_specs=out_specs, check_vma=False)
```

```python
import functools
import math

import jax
import jax.numpy as jnp
from jax import lax
from jax.experimental import pallas as pl
from jax.experimental.pallas import tpu as pltpu
from jax.sharding import PartitionSpec as P

ROWS = 512
NBIN = 512
NCOMP = 16
BANDS = 5
STAMP = 32
PIXELS = STAMP * STAMP * BANDS
NPIX = 1024
C1 = 64
C2 = 128
C3 = 256
HIDDEN = 512
CAP = 8
DEVICES = 128
SLOTS = DEVICES * CAP
SKY = 16
ZB = 8
PIX_DEV = NPIX // SKY
BIN_DEV = NBIN // ZB
MAP_ROWS = PIX_DEV * BIN_DEV // 128
BLOCK = MAP_ROWS + CAP
FRONT = 256
PITCH = 1024
EDGE_ROWS = 520

FIRST, SECOND, THIRD = 2, 2, 2

Z_TOP = 3.0
SPREAD_LOW = 0.05
SPREAD_RANGE = 0.25

F32 = jnp.float32
BF16 = jnp.bfloat16


def iota(shape, dim):
    return lax.broadcasted_iota(jnp.int32, shape, dim)


def relu16(values):
    return jnp.maximum(values, 0.0).astype(BF16)


def dot(left, right):
    return jnp.dot(left, right, preferred_element_type=F32)


def dot_nt(left, right):
    return lax.dot_general(left, right, (((1,), (1,)), ((), ())), preferred_element_type=F32)


def spread_first(w1_ref, w1_s, t1_s):
    w1_s[...] = jnp.zeros_like(w1_s)
    for kh in range(3):
        for kw in range(3):
            w1_s[kw, pl.ds(kh * BANDS, BANDS), :] = w1_ref[kh, :, kw].astype(F32)
    chan, lane = iota((C1, 512), 0), iota((C1, 512), 1)
    repeat = (chan == (lane >= 256) * 32 + (lane & 31)).astype(F32).astype(BF16)

    def row_parts(shape):
        k = iota(shape, 0)
        kh = (k >= 85).astype(jnp.int32) + (k >= 170).astype(jnp.int32)
        rem = k - 85 * kh
        col = (rem * 205) >> 10
        return k, kh, col, rem - 5 * col

    k, kh, col, band = row_parts((256, 16))
    pick = ((iota((256, 16), 1) == kh * BANDS + band) & (k < 255)).astype(F32).astype(BF16)
    k, kh, col, band = row_parts((256, 512))
    tap = col - 2 * ((iota((256, 512), 1) & 255) >> 5)
    total = jnp.zeros((256, 512), F32)
    for kw in range(3):
        lanes = dot(w1_s[kw].astype(BF16), repeat).astype(BF16)
        total = jnp.where(tap == kw, dot(pick, lanes), total)
    t1_s[1] = total.astype(BF16)
    t1_s[0] = jnp.where(col == 0, 0.0, total).astype(BF16)


def spread_second(w2_ref, w2a_s, w2b_s):
    low = iota((32, 128), 1) < 64
    zero = jnp.zeros((32, 128), F32)
    for kh in range(3):
        plain = [w2_ref[kh, kw].astype(F32) for kw in range(3)]
        swapped = [pltpu.roll(tap, 64, 1) for tap in plain]
        for g in range(2):
            lo = plain if g == 0 else swapped
            hi = swapped if g == 0 else plain
            for d in range(-1, 4):
                first = lo[d + 1] if d + 1 <= 2 else zero
                second = hi[d - 1] if d >= 1 else zero
                tile = jnp.where(low, first, second).astype(BF16)
                for q in range(2):
                    c = d + 4 * q
                    if -1 <= c <= 7:
                        at = kh * 384 + 128 + 32 * c
                        w2b_s[g, at : at + 32, 128 * q : 128 * q + 128] = tile
                    if 0 <= c <= 7:
                        at = kh * 256 + 32 * c
                        w2a_s[g, at : at + 32, 128 * q : 128 * q + 128] = tile


def spread_third(w3_ref, w3a_s, w3b_s):
    for kh in range(3):
        for kw in range(3):
            for g in range(2):
                tap = w3_ref[kh, kw, :, g * 128 : g * 128 + 128]
                for oc in range(2):
                    c = kw + 2 * oc - 1
                    at = kh * 384 + 128 + 64 * c
                    w3b_s[g, at : at + 64, 128 * oc : 128 * oc + 128] = tap
                    if c >= 0:
                        at = kh * 256 + 64 * c
                        w3a_s[g, at : at + 64, 128 * oc : 128 * oc + 128] = tap


def grouped(source, first_row, count, wa_s, wb_s, store):
    for g in range(2):
        for half in range(2):
            width = 384 if half else 256
            stack = []
            for i in range(count):
                parts = []
                for kh in range(3):
                    at = pl.multiple_of((2 * (first_row + i) + kh) * PITCH, PITCH)
                    at = pl.multiple_of(at + (g * 512 + half * 128), 128)
                    parts.append(source[:, pl.ds(at, width)])
                stack.append(jnp.concatenate(parts, axis=1))
            out = relu16(dot(jnp.concatenate(stack, axis=0), wb_s[g] if half else wa_s[g]))
            for i in range(count):
                store(first_row + i, g, half, out[i * ROWS : (i + 1) * ROWS])


def coefficients(head, live, coef_s):
    share = jax.nn.softplus(head[0:NCOMP]) + 0.1
    coef_s[0] = share * (0.5 * live / jnp.sum(share, axis=0, keepdims=True))
    coef_s[1] = Z_TOP * jax.nn.sigmoid(head[NCOMP : 2 * NCOMP])
    spread = SPREAD_LOW + SPREAD_RANGE * jax.nn.sigmoid(head[2 * NCOMP : 3 * NCOMP])
    coef_s[2] = 1.0 / (spread * math.sqrt(2.0))


def cumulate(coef_s, cdf_s, across):
    blocks = 5
    depth = EDGE_ROWS // blocks

    def mix(step, carry):
        rows = pl.multiple_of((step % blocks) * depth, 8)
        lanes = pl.ds(pl.multiple_of((step // blocks) * 128, 128), 128)
        edge = (iota((8, 128), 0) + rows).astype(F32) * (Z_TOP / NBIN)
        total = [jnp.zeros((8, 128), F32)] * (depth // 8)
        for k in range(NCOMP):
            inverse = coef_s[2, k : k + 1, lanes]
            scaled = (edge - coef_s[1, k : k + 1, lanes]) * inverse
            rise = jnp.broadcast_to(inverse * (8 * Z_TOP / NBIN), (8, 128))
            half = coef_s[0, k : k + 1, lanes]
            for i in range(depth // 8):
                total[i] = total[i] + half * lax.erf(scaled)
                scaled = scaled + rise
        cdf_s[pl.ds(rows, depth), lanes] = jnp.concatenate(total, axis=0)
        return carry

    lax.fori_loop(0, blocks * (across // 128), mix, 0)


def owner_kernel(
    counts_ref, dest_ref, pixel_ref, x_hbm, w1_ref, w2_ref, w3_ref, wd_hbm, wh_ref,
    send_ref,
    x_s, wd_s, l1_s, l2_s, l3_s, w1_s, t1_s, w2a_s, w2b_s, w3a_s, w3b_s, coef_s, cdf_s, den_s,
    sems,
):
    x_copy = pltpu.make_async_copy(x_hbm, x_s.at[:, pl.ds(FRONT, PIXELS)], sems.at[0])
    x_copy.start()
    d_copy = pltpu.make_async_copy(wd_hbm, wd_s, sems.at[1])
    d_copy.start()

    def clear(i, carry):
        rows = pl.ds(pl.multiple_of(i * 32, 32), 32)
        x_s[rows, 0:FRONT] = jnp.zeros((32, FRONT), BF16)
        l1_s[rows, 0:PITCH] = jnp.zeros((32, PITCH), BF16)
        l2_s[rows, 0:PITCH] = jnp.zeros((32, PITCH), BF16)
        return carry

    lax.fori_loop(0, ROWS // 32, clear, 0)

    def clear_weights(i, carry):
        for g in range(2):
            for wide in (w2b_s, w3b_s):
                wide[g, pl.ds(pl.multiple_of(i * 48, 48), 48), :] = jnp.zeros((48, 256), BF16)
            for narrow in (w2a_s, w3a_s):
                narrow[g, pl.ds(pl.multiple_of(i * 32, 32), 32), :] = jnp.zeros((32, 256), BF16)
        return carry

    lax.fori_loop(0, 24, clear_weights, 0)
    spread_first(w1_ref, w1_s, t1_s)
    spread_second(w2_ref, w2a_s, w2b_s)
    spread_third(w3_ref, w3a_s, w3b_s)
    x_copy.wait()

    def first(step, carry):
        for half in range(2):
            stack = []
            for i in range(FIRST):
                lanes = pl.ds(pl.multiple_of((step * FIRST + i) * 640, 128), 896)
                x = x_s[:, lanes]
                for odd in range(2):
                    start = 91 + 320 * odd + 80 * half
                    taps = [x[:, start + 160 * kh : start + 160 * kh + 85] for kh in range(3)]
                    stack.append(jnp.concatenate(taps + [jnp.zeros((ROWS, 1), BF16)], axis=1))
            out = relu16(dot(jnp.concatenate(stack, axis=0), t1_s[half]))
            for i in range(2 * FIRST):
                at = pl.multiple_of((2 * FIRST * step + i + 1) * PITCH, PITCH)
                for g in range(2):
                    lanes = pl.ds(pl.multiple_of(at + (g * 512 + half * 256), 128), 256)
                    l1_s[:, lanes] = out[i * ROWS : (i + 1) * ROWS, g * 256 : g * 256 + 256]
        return carry

    lax.fori_loop(0, STAMP // 4 // FIRST, first, 0)

    def second(step, carry):
        def store(r, g, half, out):
            at = pl.multiple_of((r + 1) * PITCH, PITCH) + (g * 512 + half * 256)
            l2_s[:, pl.ds(pl.multiple_of(at, 128), 256)] = out

        grouped(l1_s, step * SECOND, SECOND, w2a_s, w2b_s, store)
        return carry

    lax.fori_loop(0, STAMP // 4 // SECOND, second, 0)

    def third(step, carry):
        def store(r, g, half, out):
            for oc in range(2):
                at = pl.multiple_of(r * 1024, 1024) + ((2 * half + oc) * 256 + g * 128)
                l3_s[:, pl.ds(pl.multiple_of(at, 128), 128)] = out[:, oc * 128 : oc * 128 + 128]

        grouped(l2_s, step * THIRD, THIRD, w3a_s, w3b_s, store)
        return carry

    lax.fori_loop(0, STAMP // 8 // THIRD, third, 0)
    d_copy.wait()
    hidden = relu16(dot(l3_s[...], wd_s[...]))
    wh = wh_ref[...]
    head = dot_nt(hidden, jnp.concatenate([wh, wh, jnp.zeros((32, HIDDEN), BF16)], axis=0))

    count = counts_ref[0]
    high = head.astype(BF16).astype(F32)
    lane = iota((ROWS, 128), 1)
    alive = (iota((ROWS, 128), 0) < count).astype(F32)
    params = jnp.where(lane < 48, high, jnp.where(lane < 96, head - high, alive)).astype(BF16)
    dest = dest_ref[...]
    named = iota((DEVICES, ROWS), 0) == dest
    named16 = named.astype(F32).astype(BF16)
    earlier = (iota((ROWS, ROWS), 0) < iota((ROWS, ROWS), 1)).astype(F32).astype(BF16)
    rank = jnp.sum(jnp.where(named, dot(named16, earlier), 0.0), axis=0, keepdims=True)
    position = dest * CAP + rank.astype(jnp.int32)
    place = (iota((DEVICES * CAP, ROWS), 0) == position).astype(F32).astype(BF16)
    slots = dot(place, params).reshape(DEVICES, CAP, 128)
    send_ref[:, MAP_ROWS:BLOCK, :] = slots.astype(BF16)

    live = (iota((1, ROWS), 1) < count).astype(F32)
    coefficients(head.T, live, coef_s)
    cumulate(coef_s, cdf_s, ROWS)
    density = (cdf_s[1 : NBIN + 1, :] - cdf_s[0:NBIN, :]).astype(BF16).astype(F32)

    pixel = pixel_ref[...]
    odd = (pixel & 1).astype(F32)
    for j in range(ZB):
        part = density[j * BIN_DEV : (j + 1) * BIN_DEV]
        den_s[j * 128 : j * 128 + 64, :] = (part * (1.0 - odd)).astype(BF16)
        den_s[j * 128 + 64 : j * 128 + 128, :] = (part * odd).astype(BF16)
    pair = (iota((NPIX // 2, ROWS), 0) == (pixel >> 1)).astype(F32).astype(BF16)
    for q in range(ZB // 2):
        maps = dot_nt(pair, den_s[q * 256 : q * 256 + 256, :]).astype(BF16)
        for s in range(SKY):
            for j in range(2):
                send_ref[s * ZB + 2 * q + j, 0:MAP_ROWS, :] = maps[
                    s * MAP_ROWS : (s + 1) * MAP_ROWS, j * 128 : j * 128 + 128
                ]


def owner(stamps, counts, dest, pixel_ids, conv1_w, conv2_w, conv3_w, dense_w, head_w):
    vmem = pl.BlockSpec(memory_space=pltpu.VMEM)
    hbm = pl.BlockSpec(memory_space=pl.ANY)
    return pl.pallas_call(
        owner_kernel,
        out_shape=jax.ShapeDtypeStruct((DEVICES, BLOCK, 128), BF16),
        in_specs=[pl.BlockSpec(memory_space=pltpu.SMEM), vmem, vmem, hbm, vmem, vmem, vmem, hbm, vmem],
        out_specs=vmem,
        scratch_shapes=[
            pltpu.VMEM((ROWS, FRONT + PIXELS), BF16),
            pltpu.VMEM((C3 * 16, HIDDEN), BF16),
            pltpu.VMEM((ROWS, 17 * PITCH), BF16),
            pltpu.VMEM((ROWS, 9 * PITCH), BF16),
            pltpu.VMEM((ROWS, C3 * 16), BF16),
            pltpu.VMEM((3, 16, C1), F32),
            pltpu.VMEM((2, 256, 512), BF16),
            pltpu.VMEM((2, 768, 256), BF16),
            pltpu.VMEM((2, 1152, 256), BF16),
            pltpu.VMEM((2, 768, 256), BF16),
            pltpu.VMEM((2, 1152, 256), BF16),
            pltpu.VMEM((3, NCOMP, ROWS), F32),
            pltpu.VMEM((EDGE_ROWS, ROWS), F32),
            pltpu.VMEM((2 * NBIN, ROWS), BF16),
            pltpu.SemaphoreType.DMA((2,)),
        ],
        compiler_params=pltpu.CompilerParams(vmem_limit_bytes=62 * 1024 * 1024),
        cost_estimate=pl.CostEstimate(
            flops=20_000_000_000, bytes_accessed=13_000_000, transcendentals=4_300_000
        ),
        name="owner",
    )(counts, dest.reshape(1, ROWS), pixel_ids.reshape(1, ROWS), stamps,
      conv1_w.transpose(0, 2, 1, 3), conv2_w, conv3_w,
      dense_w, head_w.T)


def worker_kernel(got_ref, rows_ref, map_ref, coef_s, cdf_s):
    def add(i, total):
        part = got_ref[pl.ds(i * 8, 8), 0:MAP_ROWS, :].astype(F32)
        return total + jnp.sum(part, axis=0)

    total = lax.fori_loop(0, DEVICES // 8, add, jnp.zeros((MAP_ROWS, 128), F32))
    map_ref[pl.ds(0, PIX_DEV // 2, stride=2), :] = total[:, 0:64]
    map_ref[pl.ds(1, PIX_DEV // 2, stride=2), :] = total[:, 64:128]

    packed = got_ref[:, MAP_ROWS:BLOCK, :].astype(F32).reshape(SLOTS, 128).T
    coefficients(packed[0:48] + packed[48:96], packed[96:97], coef_s)
    cumulate(coef_s, cdf_s, SLOTS)
    same = (iota((256, 256), 0) == iota((256, 256), 1)).astype(F32).astype(BF16)
    for at in range(0, SLOTS, 256):
        part = cdf_s[1 : NBIN + 1, at : at + 256] - cdf_s[0:NBIN, at : at + 256]
        rows_ref[at : at + 256, :] = dot_nt(same, part.astype(BF16)).astype(BF16)


def worker(received):
    vmem = pl.BlockSpec(memory_space=pltpu.VMEM)
    return pl.pallas_call(
        worker_kernel,
        out_shape=(
            jax.ShapeDtypeStruct((SLOTS, NBIN), BF16),
            jax.ShapeDtypeStruct((PIX_DEV, BIN_DEV), F32),
        ),
        in_specs=[vmem],
        out_specs=(vmem, vmem),
        scratch_shapes=[pltpu.VMEM((3, NCOMP, SLOTS), F32), pltpu.VMEM((EDGE_ROWS, SLOTS), F32)],
        compiler_params=pltpu.CompilerParams(vmem_limit_bytes=32 * 1024 * 1024),
        name="worker",
    )(received)


def local(*arrays):
    send = owner(*arrays)
    received = lax.all_to_all(send, ("sky", "zb"), split_axis=0, concat_axis=0, tiled=True)
    return worker(received)


def solution(mesh):
    in_specs = (
        P(("sky", "zb"), None),
        P(("sky", "zb")),
        P(("sky", "zb"), None),
        P(("sky", "zb")),
        P(),
        P(),
        P(),
        P(),
        P(),
    )
    out_specs = (P(("sky", "zb"), None), P("sky", "zb"))
    return jax.shard_map(local, mesh=mesh, in_specs=in_specs, out_specs=out_specs, check_vma=False)
```

```python
import functools
import math

import jax
import jax.numpy as jnp
from jax import lax
from jax.experimental import pallas as pl
from jax.experimental.pallas import tpu as pltpu
from jax.sharding import PartitionSpec as P

ROWS = 512
NBIN = 512
NCOMP = 16
BANDS = 5
STAMP = 32
PIXELS = STAMP * STAMP * BANDS
NPIX = 1024
C1 = 64
C2 = 128
C3 = 256
HIDDEN = 512
CAP = 8
DEVICES = 128
SLOTS = DEVICES * CAP
SKY = 16
ZB = 8
PIX_DEV = NPIX // SKY
BIN_DEV = NBIN // ZB
MAP_ROWS = PIX_DEV * BIN_DEV // 128
BLOCK = MAP_ROWS + CAP
FRONT = 256
PITCH = 1024
EDGE_ROWS = 520

FIRST, SECOND, THIRD = 2, 2, 2
CHUNK = 640 * FIRST

Z_TOP = 3.0
SPREAD_LOW = 0.05
SPREAD_RANGE = 0.25

F32 = jnp.float32
BF16 = jnp.bfloat16


def iota(shape, dim):
    return lax.broadcasted_iota(jnp.int32, shape, dim)


def relu16(values):
    return jnp.maximum(values, 0.0).astype(BF16)


def dot(left, right):
    return jnp.dot(left, right, preferred_element_type=F32)


def dot_nt(left, right):
    return lax.dot_general(left, right, (((1,), (1,)), ((), ())), preferred_element_type=F32)


def spread_first(w1_ref, w1_s, t1_s):
    w1_s[...] = jnp.zeros_like(w1_s)
    for kh in range(3):
        for kw in range(3):
            w1_s[kw, pl.ds(kh * BANDS, BANDS), :] = w1_ref[kh, :, kw].astype(F32)
    chan, lane = iota((C1, 512), 0), iota((C1, 512), 1)
    repeat = (chan == (lane >= 256) * 32 + (lane & 31)).astype(F32).astype(BF16)

    def row_parts(shape):
        k = iota(shape, 0)
        kh = (k >= 85).astype(jnp.int32) + (k >= 170).astype(jnp.int32)
        rem = k - 85 * kh
        col = (rem * 205) >> 10
        return k, kh, col, rem - 5 * col

    k, kh, col, band = row_parts((256, 16))
    pick = ((iota((256, 16), 1) == kh * BANDS + band) & (k < 255)).astype(F32).astype(BF16)
    k, kh, col, band = row_parts((256, 512))
    tap = col - 2 * ((iota((256, 512), 1) & 255) >> 5)
    total = jnp.zeros((256, 512), F32)
    for kw in range(3):
        lanes = dot(w1_s[kw].astype(BF16), repeat).astype(BF16)
        total = jnp.where(tap == kw, dot(pick, lanes), total)
    t1_s[1] = total.astype(BF16)
    t1_s[0] = jnp.where(col == 0, 0.0, total).astype(BF16)


def spread_second(w2_ref, w2_s):
    low = iota((32, 128), 1) < 64
    zero = jnp.zeros((32, 128), F32)
    for kh in range(3):
        plain = [w2_ref[kh, kw].astype(F32) for kw in range(3)]
        swapped = [pltpu.roll(tap, 64, 1) for tap in plain]
        for g in range(2):
            lo = plain if g == 0 else swapped
            hi = swapped if g == 0 else plain
            for d in range(-1, 4):
                first = lo[d + 1] if d + 1 <= 2 else zero
                second = hi[d - 1] if d >= 1 else zero
                tile = jnp.where(low, first, second).astype(BF16)
                for q in range(2):
                    c = d + 4 * q
                    at = 128 + kh * 256 + 32 * c if c >= 0 else 96 - 32 * kh
                    if c <= 7:
                        w2_s[g, at : at + 32, 128 * q : 128 * q + 128] = tile


def spread_third(w3_ref, w3_s):
    for kh in range(3):
        for kw in range(3):
            for g in range(2):
                tap = w3_ref[kh, kw, :, g * 128 : g * 128 + 128]
                for oc in range(2):
                    c = kw + 2 * oc - 1
                    at = 256 + kh * 256 + 64 * c if c >= 0 else (64, 0, 192)[kh]
                    w3_s[g, at : at + 64, 128 * oc : 128 * oc + 128] = tap


def edge_second(tiles):
    lane = iota(tiles[0].shape, 1)
    last = jnp.where(lane >= 64, pltpu.roll(tiles[1], 96, 1), pltpu.roll(tiles[2], 64, 1))
    return [jnp.where(lane >= 96, tiles[0], last)]


def edge_third(tiles):
    lane = iota(tiles[0].shape, 1)
    return [jnp.where(lane >= 64, tiles[0], pltpu.roll(tiles[1], 64, 1)), tiles[2]]


def grouped(source, first_row, count, edge, w_s, store):
    ahead = w_s.shape[1] - 768
    for g in range(2):
        for half in range(2):
            stack = []
            for i in range(count):
                parts, tiles = [], []
                for kh in range(3):
                    at = pl.multiple_of((2 * (first_row + i) + kh) * PITCH, PITCH)
                    at = pl.multiple_of(at + (g * 512 + half * 256), 128)
                    parts.append(source[:, pl.ds(at, 256)])
                    if half:
                        tiles.append(source[:, pl.ds(pl.multiple_of(at - 128, 128), 128)])
                if half:
                    parts = edge(tiles) + parts
                stack.append(parts)
            total, at = 0.0, ahead
            for kh in range(3):
                piece = jnp.concatenate([parts[kh - 3] for parts in stack], axis=0)
                total = total + dot(piece, w_s[g, at : at + 256, :])
                at += 256
            if half:
                piece = jnp.concatenate(
                    [jnp.concatenate(parts[:-3], axis=1) for parts in stack], axis=0
                )
                first = total[:, 0:128] + dot(piece, w_s[g, 0:ahead, 0:128])
                total = jnp.concatenate([first, total[:, 128:256]], axis=1)
            out = relu16(total)
            for i in range(count):
                store(first_row + i, g, half, out[i * ROWS : (i + 1) * ROWS])


def coefficients(head, live, coef_s):
    share = jax.nn.softplus(head[0:NCOMP]) + 0.1
    coef_s[0] = share * (0.5 * live / jnp.sum(share, axis=0, keepdims=True))
    coef_s[1] = Z_TOP * jax.nn.sigmoid(head[NCOMP : 2 * NCOMP])
    spread = SPREAD_LOW + SPREAD_RANGE * jax.nn.sigmoid(head[2 * NCOMP : 3 * NCOMP])
    coef_s[2] = 1.0 / (spread * math.sqrt(2.0))


def cumulate(coef_s, cdf_s, across):
    blocks = 5
    depth = EDGE_ROWS // blocks

    def mix(step, carry):
        rows = pl.multiple_of((step % blocks) * depth, 8)
        lanes = pl.ds(pl.multiple_of((step // blocks) * 128, 128), 128)
        edge = (iota((8, 128), 0) + rows).astype(F32) * (Z_TOP / NBIN)
        total = [jnp.zeros((8, 128), F32)] * (depth // 8)
        for k in range(NCOMP):
            inverse = coef_s[2, k : k + 1, lanes]
            scaled = (edge - coef_s[1, k : k + 1, lanes]) * inverse
            rise = jnp.broadcast_to(inverse * (8 * Z_TOP / NBIN), (8, 128))
            half = coef_s[0, k : k + 1, lanes]
            for i in range(depth // 8):
                total[i] = total[i] + half * lax.erf(scaled)
                scaled = scaled + rise
        cdf_s[pl.ds(rows, depth), lanes] = jnp.concatenate(total, axis=0)
        return carry

    lax.fori_loop(0, blocks * (across // 128), mix, 0)


def owner_kernel(
    counts_ref, dest_ref, pixel_ref, x_hbm, w1_ref, w2_ref, w3_ref, wd_hbm, wh_ref,
    send_ref,
    x_s, wd_s, l1_s, l2_s, l3_s, w1_s, t1_s, w2_s, w3_s, coef_s, cdf_s, den_s,
    sems,
):
    def stamps(step):
        at = pl.multiple_of(step * CHUNK, 128)
        to = x_s.at[:, pl.ds(pl.multiple_of(FRONT + at, 128), CHUNK)]
        return pltpu.make_async_copy(x_hbm.at[:, pl.ds(at, CHUNK)], to, sems.at[step])

    for step in range(PIXELS // CHUNK):
        stamps(step).start()

    def clear(i, carry):
        rows = pl.ds(pl.multiple_of(i * 32, 32), 32)
        x_s[rows, 0:FRONT] = jnp.zeros((32, FRONT), BF16)
        l1_s[rows, 0:PITCH] = jnp.zeros((32, PITCH), BF16)
        l2_s[rows, 0:PITCH] = jnp.zeros((32, PITCH), BF16)
        return carry

    lax.fori_loop(0, ROWS // 32, clear, 0)

    def clear_weights(i, carry):
        for g in range(2):
            for weights in (w2_s, w3_s):
                weights[g, pl.ds(pl.multiple_of(i * 128, 128), 128), :] = jnp.zeros((128, 256), BF16)
        return carry

    lax.fori_loop(0, 7, clear_weights, 0)
    w3_s[:, 896:1024, :] = jnp.zeros((2, 128, 256), BF16)
    spread_first(w1_ref, w1_s, t1_s)
    spread_second(w2_ref, w2_s)
    spread_third(w3_ref, w3_s)

    def first(step, carry):
        stamps(step).wait()
        for half in range(2):
            stack = []
            for i in range(FIRST):
                lanes = pl.ds(pl.multiple_of((step * FIRST + i) * 640, 128), 896)
                x = x_s[:, lanes]
                for odd in range(2):
                    start = 91 + 320 * odd + 80 * half
                    taps = [x[:, start + 160 * kh : start + 160 * kh + 85] for kh in range(3)]
                    stack.append(jnp.concatenate(taps + [jnp.zeros((ROWS, 1), BF16)], axis=1))
            out = relu16(dot(jnp.concatenate(stack, axis=0), t1_s[half]))
            for i in range(2 * FIRST):
                at = pl.multiple_of((2 * FIRST * step + i + 1) * PITCH, PITCH)
                for g in range(2):
                    lanes = pl.ds(pl.multiple_of(at + (g * 512 + half * 256), 128), 256)
                    l1_s[:, lanes] = out[i * ROWS : (i + 1) * ROWS, g * 256 : g * 256 + 256]
        return carry

    lax.fori_loop(0, STAMP // 4 // FIRST, first, 0)
    d_copy = pltpu.make_async_copy(wd_hbm, wd_s, sems.at[PIXELS // CHUNK])
    d_copy.start()

    def second(step, carry):
        def store(r, g, half, out):
            at = pl.multiple_of((r + 1) * PITCH, PITCH) + (g * 512 + half * 256)
            l2_s[:, pl.ds(pl.multiple_of(at, 128), 256)] = out

        grouped(l1_s, step * SECOND, SECOND, edge_second, w2_s, store)
        return carry

    lax.fori_loop(0, STAMP // 4 // SECOND, second, 0)

    def third(step, carry):
        def store(r, g, half, out):
            for oc in range(2):
                at = pl.multiple_of(r * 1024, 1024) + ((2 * half + oc) * 256 + g * 128)
                l3_s[:, pl.ds(pl.multiple_of(at, 128), 128)] = out[:, oc * 128 : oc * 128 + 128]

        grouped(l2_s, step * THIRD, THIRD, edge_third, w3_s, store)
        return carry

    lax.fori_loop(0, STAMP // 8 // THIRD, third, 0)
    d_copy.wait()
    hidden = relu16(dot(l3_s[...], wd_s[...]))
    wh = wh_ref[...]
    head = dot_nt(hidden, jnp.concatenate([wh, wh, jnp.zeros((32, HIDDEN), BF16)], axis=0))

    count = counts_ref[0]
    high = head.astype(BF16).astype(F32)
    lane = iota((ROWS, 128), 1)
    alive = (iota((ROWS, 128), 0) < count).astype(F32)
    params = jnp.where(lane < 48, high, jnp.where(lane < 96, head - high, alive)).astype(BF16)
    dest = dest_ref[...]
    named = iota((DEVICES, ROWS), 0) == dest
    named16 = named.astype(F32).astype(BF16)
    earlier = (iota((ROWS, ROWS), 0) < iota((ROWS, ROWS), 1)).astype(F32).astype(BF16)
    rank = jnp.sum(jnp.where(named, dot(named16, earlier), 0.0), axis=0, keepdims=True)
    position = dest * CAP + rank.astype(jnp.int32)
    place = (iota((DEVICES * CAP, ROWS), 0) == position).astype(F32).astype(BF16)
    slots = dot(place, params).reshape(DEVICES, CAP, 128)
    send_ref[:, MAP_ROWS:BLOCK, :] = slots.astype(BF16)

    live = (iota((1, ROWS), 1) < count).astype(F32)
    coefficients(head.T, live, coef_s)
    cumulate(coef_s, cdf_s, ROWS)
    density = (cdf_s[1 : NBIN + 1, :] - cdf_s[0:NBIN, :]).astype(BF16).astype(F32)

    pixel = pixel_ref[...]
    odd = (pixel & 1).astype(F32)
    for j in range(ZB):
        part = density[j * BIN_DEV : (j + 1) * BIN_DEV]
        den_s[j * 128 : j * 128 + 64, :] = (part * (1.0 - odd)).astype(BF16)
        den_s[j * 128 + 64 : j * 128 + 128, :] = (part * odd).astype(BF16)
    pair = (iota((NPIX // 2, ROWS), 0) == (pixel >> 1)).astype(F32).astype(BF16)
    for q in range(ZB // 2):
        maps = dot_nt(pair, den_s[q * 256 : q * 256 + 256, :]).astype(BF16)
        for s in range(SKY):
            for j in range(2):
                send_ref[s * ZB + 2 * q + j, 0:MAP_ROWS, :] = maps[
                    s * MAP_ROWS : (s + 1) * MAP_ROWS, j * 128 : j * 128 + 128
                ]


def owner(stamps, counts, dest, pixel_ids, conv1_w, conv2_w, conv3_w, dense_w, head_w):
    vmem = pl.BlockSpec(memory_space=pltpu.VMEM)
    hbm = pl.BlockSpec(memory_space=pl.ANY)
    return pl.pallas_call(
        owner_kernel,
        out_shape=jax.ShapeDtypeStruct((DEVICES, BLOCK, 128), BF16),
        in_specs=[pl.BlockSpec(memory_space=pltpu.SMEM), vmem, vmem, hbm, vmem, vmem, vmem, hbm, vmem],
        out_specs=vmem,
        scratch_shapes=[
            pltpu.VMEM((ROWS, FRONT + PIXELS), BF16),
            pltpu.VMEM((C3 * 16, HIDDEN), BF16),
            pltpu.VMEM((ROWS, 17 * PITCH), BF16),
            pltpu.VMEM((ROWS, 9 * PITCH), BF16),
            pltpu.VMEM((ROWS, C3 * 16), BF16),
            pltpu.VMEM((3, 16, C1), F32),
            pltpu.VMEM((2, 256, 512), BF16),
            pltpu.VMEM((2, 896, 256), BF16),
            pltpu.VMEM((2, 1024, 256), BF16),
            pltpu.VMEM((3, NCOMP, ROWS), F32),
            pltpu.VMEM((EDGE_ROWS, ROWS), F32),
            pltpu.VMEM((2 * NBIN, ROWS), BF16),
            pltpu.SemaphoreType.DMA((PIXELS // CHUNK + 1,)),
        ],
        compiler_params=pltpu.CompilerParams(vmem_limit_bytes=62 * 1024 * 1024),
        cost_estimate=pl.CostEstimate(
            flops=20_000_000_000, bytes_accessed=13_000_000, transcendentals=4_300_000
        ),
        name="owner",
    )(counts, dest.reshape(1, ROWS), pixel_ids.reshape(1, ROWS), stamps,
      conv1_w.transpose(0, 2, 1, 3), conv2_w, conv3_w,
      dense_w, head_w.T)


def worker_kernel(got_ref, rows_ref, map_ref, coef_s, cdf_s):
    def add(i, total):
        part = got_ref[pl.ds(i * 8, 8), 0:MAP_ROWS, :].astype(F32)
        return total + jnp.sum(part, axis=0)

    total = lax.fori_loop(0, DEVICES // 8, add, jnp.zeros((MAP_ROWS, 128), F32))
    map_ref[pl.ds(0, PIX_DEV // 2, stride=2), :] = total[:, 0:64]
    map_ref[pl.ds(1, PIX_DEV // 2, stride=2), :] = total[:, 64:128]

    packed = got_ref[:, MAP_ROWS:BLOCK, :].astype(F32).reshape(SLOTS, 128).T
    coefficients(packed[0:48] + packed[48:96], packed[96:97], coef_s)
    cumulate(coef_s, cdf_s, SLOTS)
    same = (iota((256, 256), 0) == iota((256, 256), 1)).astype(F32).astype(BF16)
    for at in range(0, SLOTS, 256):
        part = cdf_s[1 : NBIN + 1, at : at + 256] - cdf_s[0:NBIN, at : at + 256]
        rows_ref[at : at + 256, :] = dot_nt(same, part.astype(BF16)).astype(BF16)


def worker(received):
    vmem = pl.BlockSpec(memory_space=pltpu.VMEM)
    return pl.pallas_call(
        worker_kernel,
        out_shape=(
            jax.ShapeDtypeStruct((SLOTS, NBIN), BF16),
            jax.ShapeDtypeStruct((PIX_DEV, BIN_DEV), F32),
        ),
        in_specs=[vmem],
        out_specs=(vmem, vmem),
        scratch_shapes=[pltpu.VMEM((3, NCOMP, SLOTS), F32), pltpu.VMEM((EDGE_ROWS, SLOTS), F32)],
        compiler_params=pltpu.CompilerParams(vmem_limit_bytes=32 * 1024 * 1024),
        name="worker",
    )(received)


def local(*arrays):
    send = owner(*arrays)
    received = lax.all_to_all(send, ("sky", "zb"), split_axis=0, concat_axis=0, tiled=True)
    return worker(received)


def solution(mesh):
    in_specs = (
        P(("sky", "zb"), None),
        P(("sky", "zb")),
        P(("sky", "zb"), None),
        P(("sky", "zb")),
        P(),
        P(),
        P(),
        P(),
        P(),
    )
    out_specs = (P(("sky", "zb"), None), P("sky", "zb"))
    return jax.shard_map(local, mesh=mesh, in_specs=in_specs, out_specs=out_specs, check_vma=False)
```

```python
import functools
import math

import jax
import jax.numpy as jnp
from jax import lax
from jax.experimental import pallas as pl
from jax.experimental.pallas import tpu as pltpu
from jax.sharding import PartitionSpec as P

ROWS = 512
NBIN = 512
NCOMP = 16
BANDS = 5
STAMP = 32
PIXELS = STAMP * STAMP * BANDS
NPIX = 1024
C1 = 64
C2 = 128
C3 = 256
HIDDEN = 512
CAP = 8
DEVICES = 128
SLOTS = DEVICES * CAP
SKY = 16
ZB = 8
PIX_DEV = NPIX // SKY
BIN_DEV = NBIN // ZB
MAP_ROWS = PIX_DEV * BIN_DEV // 128
BLOCK = MAP_ROWS + CAP
FRONT = 256
PITCH = 1024
EDGE_ROWS = 528

FIRST, SECOND, THIRD = 2, 2, 2
CHUNK = 640 * FIRST

Z_TOP = 3.0
SPREAD_LOW = 0.05
SPREAD_RANGE = 0.25

F32 = jnp.float32
BF16 = jnp.bfloat16


def iota(shape, dim):
    return lax.broadcasted_iota(jnp.int32, shape, dim)


def relu16(values):
    return jnp.maximum(values, 0.0).astype(BF16)


def dot(left, right):
    return jnp.dot(left, right, preferred_element_type=F32)


def dot_nt(left, right):
    return lax.dot_general(left, right, (((1,), (1,)), ((), ())), preferred_element_type=F32)


def spread_first(w1_ref, w1_s, t1_s):
    w1_s[...] = jnp.zeros_like(w1_s)
    for kh in range(3):
        for kw in range(3):
            w1_s[kw, pl.ds(kh * BANDS, BANDS), :] = w1_ref[kh, :, kw].astype(F32)
    chan, lane = iota((C1, 512), 0), iota((C1, 512), 1)
    repeat = (chan == (lane >= 256) * 32 + (lane & 31)).astype(F32).astype(BF16)

    def row_parts(shape):
        k = iota(shape, 0)
        kh = (k >= 85).astype(jnp.int32) + (k >= 170).astype(jnp.int32)
        rem = k - 85 * kh
        col = (rem * 205) >> 10
        return k, kh, col, rem - 5 * col

    k, kh, col, band = row_parts((256, 16))
    pick = ((iota((256, 16), 1) == kh * BANDS + band) & (k < 255)).astype(F32).astype(BF16)
    k, kh, col, band = row_parts((256, 512))
    tap = col - 2 * ((iota((256, 512), 1) & 255) >> 5)
    total = jnp.zeros((256, 512), F32)
    for kw in range(3):
        lanes = dot(w1_s[kw].astype(BF16), repeat).astype(BF16)
        total = jnp.where(tap == kw, dot(pick, lanes), total)
    t1_s[1] = total.astype(BF16)
    t1_s[0] = jnp.where(col == 0, 0.0, total).astype(BF16)


def spread_second(w2_ref, w2_s):
    low = iota((32, 128), 1) < 64
    zero = jnp.zeros((32, 128), F32)
    for kh in range(3):
        plain = [w2_ref[kh, kw].astype(F32) for kw in range(3)]
        swapped = [pltpu.roll(tap, 64, 1) for tap in plain]
        for g in range(2):
            lo = plain if g == 0 else swapped
            hi = swapped if g == 0 else plain
            for d in range(-1, 4):
                first = lo[d + 1] if d + 1 <= 2 else zero
                second = hi[d - 1] if d >= 1 else zero
                tile = jnp.where(low, first, second).astype(BF16)
                for q in range(2):
                    c = d + 4 * q
                    at = 128 + kh * 256 + 32 * c if c >= 0 else 96 - 32 * kh
                    if c <= 7:
                        w2_s[g, at : at + 32, 128 * q : 128 * q + 128] = tile


def spread_third(w3_ref, w3_s):
    for kh in range(3):
        for kw in range(3):
            for g in range(2):
                tap = w3_ref[kh, kw, :, g * 128 : g * 128 + 128]
                for oc in range(2):
                    c = kw + 2 * oc - 1
                    at = 256 + kh * 256 + 64 * c if c >= 0 else (64, 0, 192)[kh]
                    w3_s[g, at : at + 64, 128 * oc : 128 * oc + 128] = tap


def edge_second(tiles):
    lane = iota(tiles[0].shape, 1)
    last = jnp.where(lane >= 64, pltpu.roll(tiles[1], 96, 1), pltpu.roll(tiles[2], 64, 1))
    return [jnp.where(lane >= 96, tiles[0], last)]


def edge_third(tiles):
    lane = iota(tiles[0].shape, 1)
    return [jnp.where(lane >= 64, tiles[0], pltpu.roll(tiles[1], 64, 1)), tiles[2]]


def grouped(source, first_row, count, edge, w_s, store):
    ahead = w_s.shape[1] - 768
    for g in range(2):
        for half in range(2):
            stack = []
            for i in range(count):
                parts, tiles = [], []
                for kh in range(3):
                    at = pl.multiple_of((2 * (first_row + i) + kh) * PITCH, PITCH)
                    at = pl.multiple_of(at + (g * 512 + half * 256), 128)
                    parts.append(source[:, pl.ds(at, 256)])
                    if half:
                        tiles.append(source[:, pl.ds(pl.multiple_of(at - 128, 128), 128)])
                if half:
                    parts = edge(tiles) + parts
                stack.append(parts)
            total, at = 0.0, ahead
            for kh in range(3):
                piece = jnp.concatenate([parts[kh - 3] for parts in stack], axis=0)
                total = total + dot(piece, w_s[g, at : at + 256, :])
                at += 256
            if half:
                piece = jnp.concatenate(
                    [jnp.concatenate(parts[:-3], axis=1) for parts in stack], axis=0
                )
                first = total[:, 0:128] + dot(piece, w_s[g, 0:ahead, 0:128])
                total = jnp.concatenate([first, total[:, 128:256]], axis=1)
            out = relu16(total)
            for i in range(count):
                store(first_row + i, g, half, out[i * ROWS : (i + 1) * ROWS])


def coefficients(head, live, coef_s):
    share = jax.nn.softplus(head[0:NCOMP]) + 0.1
    coef_s[0] = share * (0.5 * live / jnp.sum(share, axis=0, keepdims=True))
    coef_s[1] = Z_TOP * jax.nn.sigmoid(head[NCOMP : 2 * NCOMP])
    spread = SPREAD_LOW + SPREAD_RANGE * jax.nn.sigmoid(head[2 * NCOMP : 3 * NCOMP])
    coef_s[2] = 1.0 / (spread * math.sqrt(2.0))


def cumulate(coef_s, cdf_s, across):
    blocks = 3
    depth = EDGE_ROWS // blocks

    def mix(step, carry):
        rows = pl.multiple_of((step % blocks) * depth, 8)
        lanes = pl.ds(pl.multiple_of((step // blocks) * 128, 128), 128)
        edge = (iota((8, 128), 0) + rows).astype(F32) * (Z_TOP / NBIN)
        total = [jnp.zeros((8, 128), F32)] * (depth // 8)
        for k in range(NCOMP):
            inverse = coef_s[2, k : k + 1, lanes]
            scaled = (edge - coef_s[1, k : k + 1, lanes]) * inverse
            rise = jnp.broadcast_to(inverse * (8 * Z_TOP / NBIN), (8, 128))
            half = coef_s[0, k : k + 1, lanes]
            for i in range(depth // 8):
                total[i] = total[i] + half * lax.erf(scaled)
                scaled = scaled + rise
        cdf_s[pl.ds(rows, depth), lanes] = jnp.concatenate(total, axis=0)
        return carry

    lax.fori_loop(0, blocks * (across // 128), mix, 0)


def owner_kernel(
    counts_ref, dest_ref, pixel_ref, x_hbm, w1_ref, w2_ref, w3_ref, wd_hbm, wh_ref,
    send_ref,
    x_s, wd_s, l1_s, l2_s, l3_s, w1_s, t1_s, w2_s, w3_s, coef_s, cdf_s, den_s,
    sems,
):
    def stamps(step):
        at = pl.multiple_of(step * CHUNK, 128)
        to = x_s.at[:, pl.ds(pl.multiple_of(FRONT + at, 128), CHUNK)]
        return pltpu.make_async_copy(x_hbm.at[:, pl.ds(at, CHUNK)], to, sems.at[step])

    for step in range(PIXELS // CHUNK):
        stamps(step).start()

    def clear(i, carry):
        rows = pl.ds(pl.multiple_of(i * 32, 32), 32)
        x_s[rows, 0:FRONT] = jnp.zeros((32, FRONT), BF16)
        l1_s[rows, 0:PITCH] = jnp.zeros((32, PITCH), BF16)
        l2_s[rows, 0:PITCH] = jnp.zeros((32, PITCH), BF16)
        return carry

    lax.fori_loop(0, ROWS // 32, clear, 0)

    def clear_weights(i, carry):
        for g in range(2):
            for weights in (w2_s, w3_s):
                weights[g, pl.ds(pl.multiple_of(i * 128, 128), 128), :] = jnp.zeros((128, 256), BF16)
        return carry

    lax.fori_loop(0, 7, clear_weights, 0)
    w3_s[:, 896:1024, :] = jnp.zeros((2, 128, 256), BF16)
    spread_first(w1_ref, w1_s, t1_s)
    spread_second(w2_ref, w2_s)
    spread_third(w3_ref, w3_s)

    def first(step, carry):
        stamps(step).wait()
        for half in range(2):
            stack = []
            for i in range(FIRST):
                lanes = pl.ds(pl.multiple_of((step * FIRST + i) * 640, 128), 896)
                x = x_s[:, lanes]
                for odd in range(2):
                    start = 91 + 320 * odd + 80 * half
                    taps = [x[:, start + 160 * kh : start + 160 * kh + 85] for kh in range(3)]
                    stack.append(jnp.concatenate(taps + [jnp.zeros((ROWS, 1), BF16)], axis=1))
            out = relu16(dot(jnp.concatenate(stack, axis=0), t1_s[half]))
            for i in range(2 * FIRST):
                at = pl.multiple_of((2 * FIRST * step + i + 1) * PITCH, PITCH)
                for g in range(2):
                    lanes = pl.ds(pl.multiple_of(at + (g * 512 + half * 256), 128), 256)
                    l1_s[:, lanes] = out[i * ROWS : (i + 1) * ROWS, g * 256 : g * 256 + 256]
        return carry

    lax.fori_loop(0, STAMP // 4 // FIRST, first, 0)
    d_copy = pltpu.make_async_copy(wd_hbm, wd_s, sems.at[PIXELS // CHUNK])
    d_copy.start()

    def second(step, carry):
        def store(r, g, half, out):
            at = pl.multiple_of((r + 1) * PITCH, PITCH) + (g * 512 + half * 256)
            l2_s[:, pl.ds(pl.multiple_of(at, 128), 256)] = out

        grouped(l1_s, step * SECOND, SECOND, edge_second, w2_s, store)
        return carry

    lax.fori_loop(0, STAMP // 4 // SECOND, second, 0)

    def third(step, carry):
        def store(r, g, half, out):
            for oc in range(2):
                at = pl.multiple_of(r * 1024, 1024) + ((2 * half + oc) * 256 + g * 128)
                l3_s[:, pl.ds(pl.multiple_of(at, 128), 128)] = out[:, oc * 128 : oc * 128 + 128]

        grouped(l2_s, step * THIRD, THIRD, edge_third, w3_s, store)
        return carry

    lax.fori_loop(0, STAMP // 8 // THIRD, third, 0)
    d_copy.wait()
    hidden = relu16(dot(l3_s[...], wd_s[...]))
    wh = wh_ref[...]
    head = dot_nt(hidden, jnp.concatenate([wh, wh, jnp.zeros((32, HIDDEN), BF16)], axis=0))

    count = counts_ref[0]
    high = head.astype(BF16).astype(F32)
    lane = iota((ROWS, 128), 1)
    alive = (iota((ROWS, 128), 0) < count).astype(F32)
    params = jnp.where(lane < 48, high, jnp.where(lane < 96, head - high, alive)).astype(BF16)
    dest = dest_ref[...]
    named = iota((DEVICES, ROWS), 0) == dest
    named16 = named.astype(F32).astype(BF16)
    earlier = (iota((ROWS, ROWS), 0) < iota((ROWS, ROWS), 1)).astype(F32).astype(BF16)
    rank = jnp.sum(jnp.where(named, dot(named16, earlier), 0.0), axis=0, keepdims=True)
    position = dest * CAP + rank.astype(jnp.int32)
    place = (iota((DEVICES * CAP, ROWS), 0) == position).astype(F32).astype(BF16)
    slots = dot(place, params).reshape(DEVICES, CAP, 128)
    send_ref[:, MAP_ROWS:BLOCK, :] = slots.astype(BF16)

    live = (iota((1, ROWS), 1) < count).astype(F32)
    coefficients(head.T, live, coef_s)
    cumulate(coef_s, cdf_s, ROWS)
    density = (cdf_s[1 : NBIN + 1, :] - cdf_s[0:NBIN, :]).astype(BF16).astype(F32)

    pixel = pixel_ref[...]
    odd = (pixel & 1).astype(F32)
    for j in range(ZB):
        part = density[j * BIN_DEV : (j + 1) * BIN_DEV]
        den_s[j * 128 : j * 128 + 64, :] = (part * (1.0 - odd)).astype(BF16)
        den_s[j * 128 + 64 : j * 128 + 128, :] = (part * odd).astype(BF16)
    pair = (iota((NPIX // 2, ROWS), 0) == (pixel >> 1)).astype(F32).astype(BF16)
    for q in range(ZB // 2):
        maps = dot_nt(pair, den_s[q * 256 : q * 256 + 256, :]).astype(BF16)
        for s in range(SKY):
            for j in range(2):
                send_ref[s * ZB + 2 * q + j, 0:MAP_ROWS, :] = maps[
                    s * MAP_ROWS : (s + 1) * MAP_ROWS, j * 128 : j * 128 + 128
                ]


def owner(stamps, counts, dest, pixel_ids, conv1_w, conv2_w, conv3_w, dense_w, head_w):
    vmem = pl.BlockSpec(memory_space=pltpu.VMEM)
    hbm = pl.BlockSpec(memory_space=pl.ANY)
    return pl.pallas_call(
        owner_kernel,
        out_shape=jax.ShapeDtypeStruct((DEVICES, BLOCK, 128), BF16),
        in_specs=[pl.BlockSpec(memory_space=pltpu.SMEM), vmem, vmem, hbm, vmem, vmem, vmem, hbm, vmem],
        out_specs=vmem,
        scratch_shapes=[
            pltpu.VMEM((ROWS, FRONT + PIXELS), BF16),
            pltpu.VMEM((C3 * 16, HIDDEN), BF16),
            pltpu.VMEM((ROWS, 17 * PITCH), BF16),
            pltpu.VMEM((ROWS, 9 * PITCH), BF16),
            pltpu.VMEM((ROWS, C3 * 16), BF16),
            pltpu.VMEM((3, 16, C1), F32),
            pltpu.VMEM((2, 256, 512), BF16),
            pltpu.VMEM((2, 896, 256), BF16),
            pltpu.VMEM((2, 1024, 256), BF16),
            pltpu.VMEM((3, NCOMP, ROWS), F32),
            pltpu.VMEM((EDGE_ROWS, ROWS), F32),
            pltpu.VMEM((2 * NBIN, ROWS), BF16),
            pltpu.SemaphoreType.DMA((PIXELS // CHUNK + 1,)),
        ],
        compiler_params=pltpu.CompilerParams(vmem_limit_bytes=62 * 1024 * 1024),
        cost_estimate=pl.CostEstimate(
            flops=20_000_000_000, bytes_accessed=13_000_000, transcendentals=4_300_000
        ),
        name="owner",
    )(counts, dest.reshape(1, ROWS), pixel_ids.reshape(1, ROWS), stamps,
      conv1_w.transpose(0, 2, 1, 3), conv2_w, conv3_w,
      dense_w, head_w.T)


def worker_kernel(got_ref, rows_ref, map_ref, coef_s, cdf_s):
    def add(i, total):
        part = got_ref[pl.ds(i * 8, 8), 0:MAP_ROWS, :].astype(F32)
        return total + jnp.sum(part, axis=0)

    total = lax.fori_loop(0, DEVICES // 8, add, jnp.zeros((MAP_ROWS, 128), F32))
    map_ref[pl.ds(0, PIX_DEV // 2, stride=2), :] = total[:, 0:64]
    map_ref[pl.ds(1, PIX_DEV // 2, stride=2), :] = total[:, 64:128]

    packed = got_ref[:, MAP_ROWS:BLOCK, :].astype(F32).reshape(SLOTS, 128).T
    coefficients(packed[0:48] + packed[48:96], packed[96:97], coef_s)
    cumulate(coef_s, cdf_s, SLOTS)
    same = (iota((256, 256), 0) == iota((256, 256), 1)).astype(F32).astype(BF16)
    for at in range(0, SLOTS, 256):
        part = cdf_s[1 : NBIN + 1, at : at + 256] - cdf_s[0:NBIN, at : at + 256]
        rows_ref[at : at + 256, :] = dot_nt(same, part.astype(BF16)).astype(BF16)


def worker(received):
    vmem = pl.BlockSpec(memory_space=pltpu.VMEM)
    return pl.pallas_call(
        worker_kernel,
        out_shape=(
            jax.ShapeDtypeStruct((SLOTS, NBIN), BF16),
            jax.ShapeDtypeStruct((PIX_DEV, BIN_DEV), F32),
        ),
        in_specs=[vmem],
        out_specs=(vmem, vmem),
        scratch_shapes=[pltpu.VMEM((3, NCOMP, SLOTS), F32), pltpu.VMEM((EDGE_ROWS, SLOTS), F32)],
        compiler_params=pltpu.CompilerParams(vmem_limit_bytes=32 * 1024 * 1024),
        name="worker",
    )(received)


def local(*arrays):
    send = owner(*arrays)
    received = lax.all_to_all(send, ("sky", "zb"), split_axis=0, concat_axis=0, tiled=True)
    return worker(received)


def solution(mesh):
    in_specs = (
        P(("sky", "zb"), None),
        P(("sky", "zb")),
        P(("sky", "zb"), None),
        P(("sky", "zb")),
        P(),
        P(),
        P(),
        P(),
        P(),
    )
    out_specs = (P(("sky", "zb"), None), P("sky", "zb"))
    return jax.shard_map(local, mesh=mesh, in_specs=in_specs, out_specs=out_specs, check_vma=False)
```
